32 devices in a mesh: row: 4 (over y, core), col: 8 (over z, x).
Axes of the slice: x: 2, y: 2, z: 4, core: 2. Of those that a mesh axis runs over, the one named last changes fastest.
Arguments:
- object_field: float32 [2, 512, 1024], P(None, 'row', 'col'), may hold values from -4 to 4
- probe_modes: float32 [8, 2, 128, 128], replicated, may hold values from -1.5 to 1.5
- coefficients: float32 [4, 8, 32, 8], P('row', 'col'), may hold values from -4 to 4
- offsets: int32 [4, 8, 32, 2], P('row', 'col'), may hold values from 0 to 128
- counts: int32 [4, 8], P('row', 'col'), may hold values from 16 to 32
- measured: int32 [4, 8, 32, 128, 128], P('row', 'col'), may hold values from 0 to 4095
Outputs:
- object_out: float32 [2, 512, 1024], P(None, 'row', 'col')
- modes_out: float32 [8, 2, 128, 128], replicated
- coefficients_out: float32 [4, 8, 32, 8], P('row', 'col')
The draws below stay inside these ranges and needn't reach their ends.
All inputs are finite; a program needn't handle non-finite values.
Results may differ from the reference program's by a relative error of at most 0.0003.
Values sent between devices are 32-bit elements; how exact they have to be, the bound alone decides.
A program may use at most 128 MiB of HBM per device.

```python
import jax
import jax.numpy as jnp
from jax import lax

PS = 128
MODES = 8
TILE = 128
PMAX = 32
ITERS = 2
OBJ_ROWS = 512
OBJ_COLS = 1024
N_ROW = 4
N_COL = 8


def draw_measured(key, part):
    ceilings = jax.random.randint(jax.random.fold_in(key, 11), (N_ROW, N_COL, 1, 1, 1), 512, 4097)
    return jax.random.randint(jax.random.fold_in(key, 12), (N_ROW, N_COL, PMAX, PS, PS), 0, ceilings).astype(jnp.int32)


def place_ends(drawn, own_key, least, largest):
    shape = drawn.shape
    spot = [jax.random.randint(jax.random.fold_in(own_key, axis), (), 0, shape[axis]) for axis in range(len(shape))]
    drawn = drawn.at[tuple(spot)].set(least)
    longest = shape.index(max(shape))
    spot[longest] = (spot[longest] + 1) % shape[longest]
    return drawn.at[tuple(spot)].set(largest)


def levels(key, dims, cuts, smallest, largest):
    level = 1.0
    for position, parts in cuts:
        draws = jax.random.uniform(jax.random.fold_in(jax.random.fold_in(key, 6), position), (parts,), jnp.float32, smallest / len(cuts), largest / len(cuts))
        level = level * jnp.repeat(jnp.exp(draws), dims[position] // parts).reshape((-1,) + (1,) * (len(dims) - 1 - position))
    return level


def gaussian(key, dims, spread, most, shards=(), kind=jnp.bfloat16):
    loudness = levels(key, dims, shards, -0.22, 0.18) if shards else 1.0
    result = jax.random.normal(key, dims, jnp.float32) * spread * loudness
    return jnp.minimum(jnp.maximum(result, -most), most).astype(kind)


def setup_inputs(seed: int = 0) -> dict:
    splits = jax.random.split(jax.random.key(seed), 7)
    return {
        "object_field": gaussian(splits[0], (2, OBJ_ROWS, OBJ_COLS), 0.7, 4.0, ((1, 4), (2, 8)), jnp.float32),
        "probe_modes": gaussian(splits[1], (MODES, 2, PS, PS), 0.25, 1.5, (), jnp.float32),
        "coefficients": gaussian(splits[2], (N_ROW, N_COL, PMAX, MODES), 1.0, 4.0, ((0, 4), (1, 8)), jnp.float32),
        "offsets": place_ends(jax.random.randint(splits[3], (N_ROW, N_COL, PMAX, 2), 0, TILE + 1), jax.random.fold_in(splits[3], 1), 0, TILE).astype(jnp.int32),
        "counts": place_ends(jax.random.randint(splits[4], (N_ROW, N_COL), PMAX // 2, PMAX + 1), jax.random.fold_in(splits[4], 1), PMAX // 2, PMAX).astype(jnp.int32),
        "measured": draw_measured(jax.random.fold_in(splits[6], 71), 0),
    }


amp_floor = 0.5
count_scale = 0.03125
highest = lax.Precision.HIGHEST

def position_update(patches, coef_rows, in_use, photons, probe_modes):
    obj_real = patches[:, 0]
    obj_imag = patches[:, 1]
    probes = jnp.einsum('pk,kcxy->pcxy', coef_rows, probe_modes, precision=highest)
    prb_real = probes[:, 0]
    prb_imag = probes[:, 1]
    psi_real = prb_real * obj_real - prb_imag * obj_imag
    psi_imag = prb_real * obj_imag + prb_imag * obj_real
    far_field = jnp.fft.fft2(psi_real + 1j * psi_imag, norm='ortho')
    amplitude = jnp.sqrt(far_field.real * far_field.real + far_field.imag * far_field.imag)
    target = jnp.sqrt(photons.astype(jnp.float32)) * count_scale
    corrected = far_field * (target / jnp.maximum(amplitude, amp_floor))
    back_field = jnp.fft.ifft2(corrected, norm='ortho')
    gate_grid = in_use[:, None, None]
    diff_real = (back_field.real - psi_real) * gate_grid
    diff_imag = (back_field.imag - psi_imag) * gate_grid
    grad_real = prb_real * diff_real + prb_imag * diff_imag
    grad_imag = prb_real * diff_imag - prb_imag * diff_real
    weight_grid = (prb_real * prb_real + prb_imag * prb_imag) * gate_grid
    cross_real = obj_real * diff_real + obj_imag * diff_imag
    cross_imag = obj_real * diff_imag - obj_imag * diff_real
    obj_power = (obj_real * obj_real + obj_imag * obj_imag) * gate_grid
    used_coef = coef_rows * in_use[:, None]
    moment_real = jnp.einsum('pk,pxy->kxy', used_coef, cross_real, precision=highest)
    moment_imag = jnp.einsum('pk,pxy->kxy', used_coef, cross_imag, precision=highest)
    moment_power = jnp.einsum('pk,pxy->kxy', used_coef * coef_rows, obj_power, precision=highest)
    mode_real = probe_modes[:, 0]
    mode_imag = probe_modes[:, 1]
    numerator = jnp.einsum('pxy,kxy->pk', cross_real, mode_real, precision=highest) + jnp.einsum('pxy,kxy->pk', cross_imag, mode_imag, precision=highest)
    denominator = jnp.einsum('pxy,kxy->pk', obj_power, mode_real * mode_real + mode_imag * mode_imag, precision=highest)
    coef_new = coef_rows + numerator / (denominator + 1.0)
    pieces = jnp.stack([grad_real, grad_imag, weight_grid], axis=1)
    moments = jnp.stack([moment_real, moment_imag, moment_power], axis=0)
    return (pieces, moments, coef_new)

def reference(object_field, probe_modes, coefficients, offsets, counts, measured):
    margin = PS // 2
    tile_count = N_ROW * N_COL
    coef_flat = coefficients.reshape(tile_count, PMAX, MODES)
    anchor_flat = offsets.reshape(tile_count, PMAX, 2)
    count_flat = counts.reshape(tile_count)
    photon_flat = measured.reshape(tile_count, PMAX, PS, PS)
    tile_ids = jnp.arange(tile_count, dtype=jnp.int32)
    for iteration in range(ITERS):
        padded = jnp.pad(object_field, ((0, 0), (margin, margin), (margin, margin)))
        empty_sums = jnp.zeros((3,) + padded.shape[1:], jnp.float32)
        empty_moments = jnp.zeros((3, MODES, PS, PS), jnp.float32)

        def per_tile(running, inputs):
            accumulated, moment_sum = running
            tile_id, coef_rows, anchors, count_here, photons = inputs
            row_anchor = tile_id // N_COL * TILE
            col_anchor = tile_id % N_COL * TILE
            row_index = (anchors[:, 0] + row_anchor).astype(jnp.int32)
            col_index = (anchors[:, 1] + col_anchor).astype(jnp.int32)
            patches = jax.vmap(lambda top_row, left_col: lax.dynamic_slice(padded, (jnp.int32(0), top_row, left_col), (2, PS, PS)))(row_index, col_index)
            in_use = (jnp.arange(PMAX, dtype=jnp.int32) < count_here).astype(jnp.float32)
            pieces, moments, coef_new = position_update(patches, coef_rows, in_use, photons, probe_modes)

            def add_piece(slot_index, totals):
                corner = (jnp.int32(0), row_index[slot_index], col_index[slot_index])
                current = lax.dynamic_slice(totals, corner, (3, PS, PS))
                return lax.dynamic_update_slice(totals, current + pieces[slot_index], corner)
            accumulated = lax.fori_loop(0, PMAX, add_piece, accumulated)
            return ((accumulated, moment_sum + moments), coef_new)
        (accumulated, moment_sum), coef_flat = lax.scan(per_tile, (empty_sums, empty_moments), (tile_ids, coef_flat, anchor_flat, count_flat, photon_flat))
        interior = accumulated[:, margin:margin + OBJ_ROWS, margin:margin + OBJ_COLS]
        object_field = object_field + interior[0:2] / (interior[2:3] + 1.0)
        probe_modes = probe_modes + jnp.stack([moment_sum[0], moment_sum[1]], axis=1) / (moment_sum[2][:, None] + 1.0)
    return (object_field, probe_modes, coef_flat.reshape(coefficients.shape))
```

```python
import functools
import math

import jax
import jax.numpy as jnp
import numpy as np
from jax import lax
from jax.experimental import pallas as pl
from jax.experimental.pallas import tpu as pltpu
from jax.sharding import PartitionSpec as P

ITERS = 2
GROUP = 4
VMEM_LIMIT = 48 * 1024 * 1024

amp_floor = 0.5
count_scale = 0.03125


def extended_2(block, sides, width):
    for axis, dim in sides:
        count = lax.axis_size(axis)
        forward = [(i, i + 1) for i in range(count - 1)]
        backward = [(target, source) for source, target in forward]
        low = lax.ppermute(
            lax.slice_in_dim(block, block.shape[dim] - width, None, axis=dim), axis, forward
        )
        high = lax.ppermute(lax.slice_in_dim(block, 0, width, axis=dim), axis, backward)
        block = jnp.concatenate([low, block, high], axis=dim)
    return block


def halves(values):
    high = values.astype(jnp.bfloat16)
    low = (values - high.astype(jnp.float32)).astype(jnp.bfloat16)
    return high, low


def dft_tables(length):
    ramp = np.arange(length)
    angles = (ramp[:, None] * ramp[None, :] % length) * (2.0 * math.pi / length)
    cos = np.cos(angles) / math.sqrt(length)
    sin = -np.sin(angles) / math.sqrt(length)
    tables = []
    for part in (sin, -sin):
        right = jnp.asarray(np.block([[cos, part], [-part, cos]]), jnp.float32)
        left = jnp.asarray(np.block([[cos, -part], [part, cos]]), jnp.float32)
        high, low = halves(right)
        tables.append(jnp.concatenate([high, low, high], axis=0))
        high, low = halves(left)
        tables.append(jnp.concatenate([high, low, high], axis=1))
    return tables


def right_apply(values, table):
    high, low = halves(values)
    return jnp.dot(
        jnp.concatenate([high, high, low], axis=1), table, preferred_element_type=jnp.float32
    )


def left_apply(table, values):
    high, low = halves(values)
    return jnp.dot(
        table, jnp.concatenate([high, high, low], axis=0), preferred_element_type=jnp.float32
    )


def positions_kernel(
    count_ref, offs_ref, coef_ref, ext_ref, modes_ref, photon_ref, fr_ref, fl_ref, br_ref, bl_ref,
    acc_ref, mom_ref, num_ref, den_ref, obj_s, prb_s, psi_s, cross_s, power_s,
):
    modes, _, size, _ = modes_ref.shape
    extent = 2 * size
    step = 16
    chunks = size // step
    acc_ref[...] = jnp.zeros_like(acc_ref)
    mom_ref[...] = jnp.zeros_like(mom_ref)
    num_ref[...] = jnp.zeros_like(num_ref)
    den_ref[...] = jnp.zeros_like(den_ref)
    for k in range(modes):
        re, im = modes_ref[k, 0], modes_ref[k, 1]
        power_s[k] = re * re + im * im
    lane = lax.broadcasted_iota(jnp.int32, (size, size), 1)
    live = count_ref[0]

    def group(number, carry):
        first = number * GROUP
        weights = [[coef_ref[first + g, k] for k in range(modes)] for g in range(GROUP)]
        gates = [jnp.where(first + g < live, 1.0, 0.0).astype(jnp.float32) for g in range(GROUP)]
        corners = [(offs_ref[first + g, 0], offs_ref[first + g, 1]) for g in range(GROUP)]

        def probe_rows(chunk, carry):
            rows = pl.ds(pl.multiple_of(chunk * 8, 8), 8)
            for comp in range(2):
                parts = [modes_ref[k, comp, rows, :] for k in range(modes)]
                for g in range(GROUP):
                    total = weights[g][0] * parts[0]
                    for k in range(1, modes):
                        total = total + weights[g][k] * parts[k]
                    prb_s[g, comp, rows, :] = total
            return carry

        lax.fori_loop(0, size // 8, probe_rows, 0, unroll=2)

        for g in range(GROUP):
            top, left = corners[g]
            for comp in range(2):
                low = ext_ref[pl.ds(2 * comp * extent + top, size), :]
                high = ext_ref[pl.ds((2 * comp + 1) * extent + top, size), :]
                picked = jnp.where(lane >= left, low, high)
                obj_s[g, comp] = pltpu.roll(picked, lax.rem(size - left, size), 1)
            pr, pi, ore, oim = prb_s[g, 0], prb_s[g, 1], obj_s[g, 0], obj_s[g, 1]
            psi_s[g, :, :size] = pr * ore - pi * oim
            psi_s[g, :, size:] = pr * oim + pi * ore

        rowed = right_apply(psi_s[...].reshape(GROUP * size, 2 * size), fr_ref[...])
        for pair in range(GROUP // 2):
            one = rowed[2 * pair * size : (2 * pair + 1) * size]
            two = rowed[(2 * pair + 1) * size : (2 * pair + 2) * size]
            stacked = jnp.concatenate(
                [
                    jnp.concatenate([one[:, :size], two[:, :size]], axis=1),
                    jnp.concatenate([one[:, size:], two[:, size:]], axis=1),
                ],
                axis=0,
            )
            far = left_apply(fl_ref[...], stacked)
            far_real, far_imag = far[:size], far[size:]
            photons = jnp.concatenate(
                [photon_ref[first + 2 * pair], photon_ref[first + 2 * pair + 1]], axis=1
            )
            target = jnp.sqrt(photons.astype(jnp.float32)) * count_scale
            square = far_real * far_real + far_imag * far_imag
            scaling = target * lax.rsqrt(jnp.maximum(square, amp_floor * amp_floor))
            fixed = jnp.concatenate([far_real * scaling, far_imag * scaling], axis=0)
            near = left_apply(bl_ref[...], fixed)
            for half in range(2):
                g = 2 * pair + half
                cols = slice(half * size, (half + 1) * size)
                mixed = jnp.concatenate([near[:size, cols], near[size:, cols]], axis=1)
                back = right_apply(mixed, br_ref[...])
                diff = (back - psi_s[g]) * gates[g]
                dr, di = diff[:, :size], diff[:, size:]
                pr, pi, ore, oim = prb_s[g, 0], prb_s[g, 1], obj_s[g, 0], obj_s[g, 1]
                cross_s[g, 0] = ore * dr + oim * di
                cross_s[g, 1] = ore * di - oim * dr
                cross_s[g, 2] = (ore * ore + oim * oim) * gates[g]
                top, left = corners[g]
                pieces = (
                    pr * dr + pi * di,
                    pr * di - pi * dr,
                    (pr * pr + pi * pi) * gates[g],
                )
                inside = lane >= left
                for comp in range(3):
                    moved = pltpu.roll(pieces[comp], lax.rem(left, size), 1)
                    low = pl.ds(2 * comp * extent + top, size)
                    high = pl.ds((2 * comp + 1) * extent + top, size)
                    acc_ref[low, :] += jnp.where(inside, moved, 0.0)
                    acc_ref[high, :] += jnp.where(inside, 0.0, moved)

        def mode_sums(k, carry):
            used = [coef_ref[first + g, k] for g in range(GROUP)]

            def rows_sums(chunk, sums):
                rows = pl.ds(pl.multiple_of(chunk * step, step), step)
                re, im, power = modes_ref[k, 0, rows, :], modes_ref[k, 1, rows, :], power_s[k, rows, :]
                totals = [mom_ref[c, k, rows, :] for c in range(3)]
                new = []
                for g in range(GROUP):
                    cr, ci, cp = (cross_s[g, c, rows, :] for c in range(3))
                    totals[0] = totals[0] + used[g] * cr
                    totals[1] = totals[1] + used[g] * ci
                    totals[2] = totals[2] + (used[g] * used[g]) * cp
                    num = (cr * re + ci * im).reshape(step // 8, 8, size).sum(axis=0)
                    den = (cp * power).reshape(step // 8, 8, size).sum(axis=0)
                    new.append((sums[g][0] + num, sums[g][1] + den))
                for c in range(3):
                    mom_ref[c, k, rows, :] = totals[c]
                return tuple(new)

            zero = jnp.zeros((8, size), jnp.float32)
            sums = lax.fori_loop(
                0, chunks, rows_sums, tuple((zero, zero) for _ in range(GROUP)), unroll=4
            )
            for g in range(GROUP):
                num_ref[first + g, pl.ds(k, 1), :] = sums[g][0].sum(axis=0, keepdims=True)
                den_ref[first + g, pl.ds(k, 1), :] = sums[g][1].sum(axis=0, keepdims=True)
            return carry

        lax.fori_loop(0, modes, mode_sums, 0)
        return carry

    lax.fori_loop(0, (live + GROUP - 1) // GROUP, group, 0)


def positions_call(count, offs, coef, ext, modes, photons, tables):
    slots, kinds = coef.shape
    size = modes.shape[-1]
    extent = 2 * size
    smem = pl.BlockSpec(memory_space=pltpu.SMEM)
    vmem = pl.BlockSpec(memory_space=pltpu.VMEM)
    f32 = jnp.float32
    return pl.pallas_call(
        positions_kernel,
        out_shape=(
            jax.ShapeDtypeStruct((6 * extent, size), f32),
            jax.ShapeDtypeStruct((3, kinds, size, size), f32),
            jax.ShapeDtypeStruct((slots, kinds, size), f32),
            jax.ShapeDtypeStruct((slots, kinds, size), f32),
        ),
        in_specs=[smem] * 3 + [vmem] * 7,
        out_specs=(vmem,) * 4,
        scratch_shapes=[
            pltpu.VMEM((GROUP, 2, size, size), f32),
            pltpu.VMEM((GROUP, 2, size, size), f32),
            pltpu.VMEM((GROUP, size, 2 * size), f32),
            pltpu.VMEM((GROUP, 3, size, size), f32),
            pltpu.VMEM((kinds, size, size), f32),
        ],
        compiler_params=pltpu.CompilerParams(vmem_limit_bytes=VMEM_LIMIT),
        name="positions",
    )(count, offs, coef, ext, modes, photons, *tables)


def fold_edges(padded, margin):
    tile_width = padded.shape[1] - 4 * margin
    lower_edge = 2 * margin
    upper_edge = tile_width + 2 * margin
    outer_edge = tile_width + 3 * margin
    inner_end = tile_width - margin
    interior = padded[:, lower_edge:upper_edge, lower_edge:upper_edge]
    interior = interior.at[:, :margin, :].add(padded[:, :margin, lower_edge:upper_edge])
    interior = interior.at[:, inner_end:, :].add(padded[:, outer_edge:, lower_edge:upper_edge])
    interior = interior.at[:, :, :margin].add(padded[:, lower_edge:upper_edge, :margin])
    interior = interior.at[:, :, inner_end:].add(padded[:, lower_edge:upper_edge, outer_edge:])
    interior = interior.at[:, :margin, :margin].add(padded[:, :margin, :margin])
    interior = interior.at[:, :margin, inner_end:].add(padded[:, :margin, outer_edge:])
    interior = interior.at[:, inner_end:, :margin].add(padded[:, outer_edge:, :margin])
    interior = interior.at[:, inner_end:, inner_end:].add(padded[:, outer_edge:, outer_edge:])
    return interior


def folded(block, sides, width):
    for axis, dim in sides:
        count = lax.axis_size(axis)
        forward = [(i, i + 1) for i in range(count - 1)]
        backward = [(target, source) for source, target in forward]
        size = block.shape[dim] - 2 * width
        low = lax.ppermute(lax.slice_in_dim(block, 0, width, axis=dim), axis, backward)
        high = lax.ppermute(lax.slice_in_dim(block, size + width, None, axis=dim), axis, forward)
        inner = lax.slice_in_dim(block, width, size + width, axis=dim)
        first = lax.slice_in_dim(inner, 0, width, axis=dim) + high
        last = lax.slice_in_dim(inner, size - width, None, axis=dim) + low
        middle = lax.slice_in_dim(inner, width, size - width, axis=dim)
        block = jnp.concatenate([first, middle, last], axis=dim)
    return block


def shards(object_field, probe_modes, coefficients, offsets, counts, measured):
    size = measured.shape[-1]
    margin = size // 2
    extent = object_field.shape[1] + size
    tables = dft_tables(size)
    coef = coefficients[0, 0]
    sides = (("row", 1), ("col", 2))
    for iteration in range(ITERS):
        extended = extended_2(object_field, sides, margin)
        ext = extended.reshape(2, extent, 2, size).transpose(0, 2, 1, 3).reshape(-1, size)
        acc, moments, num, den = positions_call(
            counts[0], offsets[0, 0], coef, ext, probe_modes, measured[0, 0], tables
        )
        coef = coef + num.sum(axis=-1) / (den.sum(axis=-1) + 1.0)
        acc = acc.reshape(3, 2, extent, size).transpose(0, 2, 1, 3).reshape(3, extent, extent)
        interior = folded(acc, sides, margin)
        object_field = object_field + interior[0:2] / (interior[2:3] + 1.0)
        totals = lax.psum(moments, ("row", "col"))
        probe_modes = probe_modes + jnp.stack([totals[0], totals[1]], axis=1) / (
            totals[2][:, None] + 1.0
        )
    return (object_field, probe_modes, coef[None, None])


def solution(mesh):
    placed = (
        P(None, "row", "col"),
        P(),
        P("row", "col", None, None),
        P("row", "col", None, None),
        P("row", "col"),
        P("row", "col", None, None, None),
    )
    return jax.shard_map(
        shards,
        mesh=mesh,
        in_specs=placed,
        out_specs=(P(None, "row", "col"), P(), P("row", "col", None, None)),
        check_vma=False,
    )
```

```python
import functools
import math

import jax
import jax.numpy as jnp
import numpy as np
from jax import lax
from jax.experimental import pallas as pl
from jax.experimental.pallas import tpu as pltpu
from jax.sharding import PartitionSpec as P

ITERS = 2
GROUP = 4
VMEM_LIMIT = 48 * 1024 * 1024

amp_floor = 0.5
count_scale = 0.03125


def halves(values):
    high = values.astype(jnp.bfloat16)
    low = (values - high.astype(jnp.float32)).astype(jnp.bfloat16)
    return high, low


def dft_tables(length):
    ramp = np.arange(length)
    angles = (ramp[:, None] * ramp[None, :] % length) * (2.0 * math.pi / length)
    cos = np.cos(angles) / math.sqrt(length)
    sin = -np.sin(angles) / math.sqrt(length)
    tables = []
    for part in (sin, -sin):
        right = jnp.asarray(np.block([[cos, part], [-part, cos]]), jnp.float32)
        left = jnp.asarray(np.block([[cos, -part], [part, cos]]), jnp.float32)
        high, low = halves(right)
        tables.append(jnp.concatenate([high, low, high], axis=0))
        high, low = halves(left)
        tables.append(jnp.concatenate([high, low, high], axis=1))
    return tables


def right_apply(values, table):
    high, low = halves(values)
    return jnp.dot(
        jnp.concatenate([high, high, low], axis=1), table, preferred_element_type=jnp.float32
    )


def left_apply(table, values):
    high, low = halves(values)
    return jnp.dot(
        table, jnp.concatenate([high, high, low], axis=0), preferred_element_type=jnp.float32
    )


def positions_kernel(
    count_ref, offs_ref, coef_ref, ext_ref, modes_ref, photon_ref, fr_ref, fl_ref, br_ref, bl_ref,
    acc_ref, mom_ref, num_ref, den_ref, obj_s, prb_s, psi_s, cross_s, power_s,
):
    _, modes, size, _ = modes_ref.shape
    extent = 2 * size
    step = 16
    chunks = size // step
    acc_ref[...] = jnp.zeros_like(acc_ref)
    mom_ref[...] = jnp.zeros_like(mom_ref)
    num_ref[...] = jnp.zeros_like(num_ref)
    den_ref[...] = jnp.zeros_like(den_ref)
    for k in range(modes):
        re, im = modes_ref[0, k], modes_ref[1, k]
        power_s[k] = re * re + im * im
    lane = lax.broadcasted_iota(jnp.int32, (size, size), 1)
    live = count_ref[0]

    def group(number, carry):
        first = number * GROUP
        weights = [[coef_ref[first + g, k] for k in range(modes)] for g in range(GROUP)]
        gates = [jnp.where(first + g < live, 1.0, 0.0).astype(jnp.float32) for g in range(GROUP)]
        corners = [(offs_ref[first + g, 0], offs_ref[first + g, 1]) for g in range(GROUP)]

        def probe_rows(chunk, carry):
            rows = pl.ds(pl.multiple_of(chunk * 8, 8), 8)
            for comp in range(2):
                parts = [modes_ref[comp, k, rows, :] for k in range(modes)]
                for g in range(GROUP):
                    total = weights[g][0] * parts[0]
                    for k in range(1, modes):
                        total = total + weights[g][k] * parts[k]
                    prb_s[g, comp, rows, :] = total
            return carry

        lax.fori_loop(0, size // 8, probe_rows, 0, unroll=2)

        for g in range(GROUP):
            top, left = corners[g]
            for comp in range(2):
                low = ext_ref[pl.ds(2 * comp * extent + top, size), :]
                high = ext_ref[pl.ds((2 * comp + 1) * extent + top, size), :]
                picked = jnp.where(lane >= left, low, high)
                obj_s[g, comp] = pltpu.roll(picked, lax.rem(size - left, size), 1)
            pr, pi, ore, oim = prb_s[g, 0], prb_s[g, 1], obj_s[g, 0], obj_s[g, 1]
            psi_s[g, :, :size] = pr * ore - pi * oim
            psi_s[g, :, size:] = pr * oim + pi * ore

        rowed = right_apply(psi_s[...].reshape(GROUP * size, 2 * size), fr_ref[...])
        for pair in range(GROUP // 2):
            one = rowed[2 * pair * size : (2 * pair + 1) * size]
            two = rowed[(2 * pair + 1) * size : (2 * pair + 2) * size]
            stacked = jnp.concatenate(
                [
                    jnp.concatenate([one[:, :size], two[:, :size]], axis=1),
                    jnp.concatenate([one[:, size:], two[:, size:]], axis=1),
                ],
                axis=0,
            )
            far = left_apply(fl_ref[...], stacked)
            far_real, far_imag = far[:size], far[size:]
            photons = jnp.concatenate(
                [photon_ref[first + 2 * pair], photon_ref[first + 2 * pair + 1]], axis=1
            )
            target = jnp.sqrt(photons.astype(jnp.float32)) * count_scale
            square = far_real * far_real + far_imag * far_imag
            scaling = target * lax.rsqrt(jnp.maximum(square, amp_floor * amp_floor))
            fixed = jnp.concatenate([far_real * scaling, far_imag * scaling], axis=0)
            near = left_apply(bl_ref[...], fixed)
            for half in range(2):
                g = 2 * pair + half
                cols = slice(half * size, (half + 1) * size)
                mixed = jnp.concatenate([near[:size, cols], near[size:, cols]], axis=1)
                back = right_apply(mixed, br_ref[...])
                diff = (back - psi_s[g]) * gates[g]
                dr, di = diff[:, :size], diff[:, size:]
                pr, pi, ore, oim = prb_s[g, 0], prb_s[g, 1], obj_s[g, 0], obj_s[g, 1]
                cross_s[g, 0] = ore * dr + oim * di
                cross_s[g, 1] = ore * di - oim * dr
                cross_s[g, 2] = (ore * ore + oim * oim) * gates[g]
                top, left = corners[g]
                pieces = (
                    pr * dr + pi * di,
                    pr * di - pi * dr,
                    (pr * pr + pi * pi) * gates[g],
                )
                inside = lane >= left
                for comp in range(3):
                    moved = pltpu.roll(pieces[comp], lax.rem(left, size), 1)
                    low = pl.ds(2 * comp * extent + top, size)
                    high = pl.ds((2 * comp + 1) * extent + top, size)
                    acc_ref[low, :] += jnp.where(inside, moved, 0.0)
                    acc_ref[high, :] += jnp.where(inside, 0.0, moved)

        def mode_sums(k, carry):
            used = [coef_ref[first + g, k] for g in range(GROUP)]

            def rows_sums(chunk, sums):
                rows = pl.ds(pl.multiple_of(chunk * step, step), step)
                re, im, power = modes_ref[0, k, rows, :], modes_ref[1, k, rows, :], power_s[k, rows, :]
                totals = [mom_ref[c, k, rows, :] for c in range(3)]
                new = []
                for g in range(GROUP):
                    cr, ci, cp = (cross_s[g, c, rows, :] for c in range(3))
                    totals[0] = totals[0] + used[g] * cr
                    totals[1] = totals[1] + used[g] * ci
                    totals[2] = totals[2] + (used[g] * used[g]) * cp
                    num = (cr * re + ci * im).reshape(step // 8, 8, size).sum(axis=0)
                    den = (cp * power).reshape(step // 8, 8, size).sum(axis=0)
                    new.append((sums[g][0] + num, sums[g][1] + den))
                for c in range(3):
                    mom_ref[c, k, rows, :] = totals[c]
                return tuple(new)

            zero = jnp.zeros((8, size), jnp.float32)
            sums = lax.fori_loop(
                0, chunks, rows_sums, tuple((zero, zero) for _ in range(GROUP)), unroll=4
            )
            for g in range(GROUP):
                num_ref[first + g, pl.ds(k, 1), :] = sums[g][0].sum(axis=0, keepdims=True)
                den_ref[first + g, pl.ds(k, 1), :] = sums[g][1].sum(axis=0, keepdims=True)
            return carry

        lax.fori_loop(0, modes, mode_sums, 0)
        return carry

    lax.fori_loop(0, (live + GROUP - 1) // GROUP, group, 0)


def positions_call(count, offs, coef, ext, modes, photons, tables):
    slots, kinds = coef.shape
    size = modes.shape[-1]
    extent = 2 * size
    smem = pl.BlockSpec(memory_space=pltpu.SMEM)
    vmem = pl.BlockSpec(memory_space=pltpu.VMEM)
    f32 = jnp.float32
    return pl.pallas_call(
        positions_kernel,
        out_shape=(
            jax.ShapeDtypeStruct((6 * extent, size), f32),
            jax.ShapeDtypeStruct((3, kinds, size, size), f32),
            jax.ShapeDtypeStruct((slots, kinds, size), f32),
            jax.ShapeDtypeStruct((slots, kinds, size), f32),
        ),
        in_specs=[smem] * 3 + [vmem] * 7,
        out_specs=(vmem,) * 4,
        scratch_shapes=[
            pltpu.VMEM((GROUP, 2, size, size), f32),
            pltpu.VMEM((GROUP, 2, size, size), f32),
            pltpu.VMEM((GROUP, size, 2 * size), f32),
            pltpu.VMEM((GROUP, 3, size, size), f32),
            pltpu.VMEM((kinds, size, size), f32),
        ],
        compiler_params=pltpu.CompilerParams(vmem_limit_bytes=VMEM_LIMIT),
        name="positions",
    )(count, offs, coef, ext, modes, photons, *tables)


def edge_copies(src_low, dst_low, src_high, dst_high, axis, sems):
    place = {name: lax.axis_index(name) for name in ("row", "col")}
    here, count = place[axis], lax.axis_size(axis)
    send_sem, recv_sem, first = sems
    copies = []
    for number, (src, dst, to) in enumerate(
        ((src_low, dst_low, jnp.maximum(here - 1, 0)), (src_high, dst_high, jnp.minimum(here + 1, count - 1)))
    ):
        target = dict(place)
        target[axis] = to
        copies.append(
            pltpu.make_async_remote_copy(
                src_ref=src,
                dst_ref=dst,
                send_sem=send_sem.at[first + number],
                recv_sem=recv_sem.at[first + number],
                device_id=(target["row"], target["col"]),
                device_id_type=pl.DeviceIdType.MESH,
            )
        )
    below, above = here > 0, here < count - 1

    def start():
        pl.when(below)(copies[0].start)
        pl.when(above)(copies[1].start)

    def arrive():
        pl.when(above)(copies[0].wait_recv)
        pl.when(below)(copies[1].wait_recv)

    def finish():
        pl.when(below)(copies[0].wait_send)
        pl.when(above)(copies[1].wait_send)

    return start, arrive, finish


def exchange_kernel(has_fold, has_halo, *refs):
    refs = list(refs)
    obj_ref = refs.pop(0)
    if has_fold:
        acc_ref, mom_ref, modes_ref = refs[:3]
        obj_out, modes_out = refs[3:5]
        refs = refs[5:]
    if has_halo:
        ext_ref = refs.pop(0)
    send_sem, recv_sem = refs[:2]
    refs = refs[2:]
    if has_halo:
        q_s, qlow_s, qhigh_s = refs[:3]
        refs = refs[3:]
    if has_fold:
        up_s, down_s, mid_s, fromlow_s, fromhigh_s, buf1, sum1, buf2, sum2, buf3 = refs

    row, col = lax.axis_index("row"), lax.axis_index("col")
    rows_n, cols_n = lax.axis_size("row"), lax.axis_size("col")
    size = obj_ref.shape[-1]
    margin = size // 2
    tile_end = margin + size

    barrier = pltpu.get_barrier_semaphore()
    for step in range(1, rows_n):
        pl.semaphore_signal(
            barrier, inc=1, device_id=(lax.rem(row + step, rows_n), col), device_id_type=pl.DeviceIdType.MESH
        )
    for step in range(1, cols_n):
        pl.semaphore_signal(
            barrier, inc=1, device_id=(row, lax.rem(col + step, cols_n)), device_id_type=pl.DeviceIdType.MESH
        )
    pl.semaphore_wait(barrier, rows_n + cols_n - 2)

    used = [0]

    def take(count):
        first = used[0]
        used[0] += count
        return first

    def copy(src, dst, device, number):
        return pltpu.make_async_remote_copy(
            src_ref=src,
            dst_ref=dst,
            send_sem=send_sem.at[number],
            recv_sem=recv_sem.at[number],
            device_id=device,
            device_id_type=pl.DeviceIdType.MESH,
        )

    finishing = []
    lane = lax.broadcasted_iota(jnp.int32, (size, size), 1)
    upper = lane >= margin

    if has_fold:
        total_rows = mom_ref.shape[1]
        core, line, lines = lax.rem(row, 2), row // 2, rows_n // 2
        half_rows = total_rows // 2
        line_rows = half_rows // lines
        own_rows = line_rows // cols_n
        half_at = pl.multiple_of(core * half_rows, half_rows)
        other_at = pl.multiple_of((1 - core) * half_rows, half_rows)
        line_at = pl.multiple_of(half_at + line * line_rows, line_rows)
        own_at = pl.multiple_of(line_at + col * own_rows, own_rows)
        partner = (line * 2 + 1 - core, col)

        pair = copy(mom_ref.at[:, pl.ds(other_at, half_rows), :], buf1, partner, take(1))
        pair.start()
        start, arrive, finish = edge_copies(
            acc_ref.at[:, pl.ds(0, margin), :], down_s,
            acc_ref.at[:, pl.ds(tile_end, margin), :], up_s,
            "row", (send_sem, recv_sem, take(2)),
        )

        @pl.when(row == 0)
        def _():
            up_s[...] = jnp.zeros_like(up_s)

        @pl.when(row == rows_n - 1)
        def _():
            down_s[...] = jnp.zeros_like(down_s)

        @pl.when(col == 0)
        def _():
            fromlow_s[...] = jnp.zeros_like(fromlow_s)

        @pl.when(col == cols_n - 1)
        def _():
            fromhigh_s[...] = jnp.zeros_like(fromhigh_s)

        start()
        finishing += [finish, pair.wait_send]

        pair.wait_recv()
        sum1[...] = mom_ref[:, pl.ds(half_at, half_rows), :] + buf1[...]
        first = take(lines - 1)
        line_copies = []
        for step in range(1, lines):
            to = lax.rem(line + step, lines)
            at = pl.multiple_of(to * line_rows, line_rows)
            line_copies.append(
                copy(sum1.at[:, pl.ds(at, line_rows), :], buf2.at[step - 1], (to * 2 + core, col), first + step - 1)
            )
            line_copies[-1].start()

        arrive()
        for comp in range(3):
            for half in range(2):
                plane = 2 * comp + half
                mid_s[half, comp, :margin, :] = acc_ref[plane, margin:size, :] + up_s[plane]
                mid_s[half, comp, margin:, :] = acc_ref[plane, size:tile_end, :] + down_s[plane]
        start, arrive, finish = edge_copies(
            mid_s.at[0], fromhigh_s, mid_s.at[1], fromlow_s, "col", (send_sem, recv_sem, take(2))
        )
        start()
        finishing.append(finish)

        total = sum1[:, pl.ds(pl.multiple_of(line * line_rows, line_rows), line_rows), :]
        for step in range(1, lines):
            line_copies[step - 1].wait_recv()
            total = total + buf2[step - 1]
        sum2[...] = total
        first = take(cols_n - 1)
        col_copies = []
        for step in range(1, cols_n):
            to = lax.rem(col + step, cols_n)
            at = pl.multiple_of(to * own_rows, own_rows)
            col_copies.append(copy(sum2.at[:, pl.ds(at, own_rows), :], buf3.at[step - 1], (row, to), first + step - 1))
            col_copies[-1].start()
        finishing += [c.wait_send for c in line_copies + col_copies]

        arrive()
        parts = [
            jnp.where(upper, mid_s[0, c] + fromlow_s[c], mid_s[1, c] + fromhigh_s[c]) for c in range(3)
        ]
        for c in range(2):
            new = pltpu.roll(obj_ref[c], margin, 1) + parts[c] / (parts[2] + 1.0)
            if has_halo:
                q_s[c] = new
            obj_out[c] = pltpu.roll(new, margin, 1)
    else:
        for c in range(2):
            q_s[c] = pltpu.roll(obj_ref[c], margin, 1)

    if has_halo:

        @pl.when(col == 0)
        def _():
            qlow_s[...] = jnp.zeros_like(qlow_s)

        @pl.when(col == cols_n - 1)
        def _():
            qhigh_s[...] = jnp.zeros_like(qhigh_s)

        start, arrive, finish = edge_copies(q_s, qhigh_s, q_s, qlow_s, "col", (send_sem, recv_sem, take(2)))
        start()
        finishing.append(finish)

    if has_fold:
        total = sum2[:, pl.ds(pl.multiple_of(col * own_rows, own_rows), own_rows), :]
        for step in range(1, cols_n):
            col_copies[step - 1].wait_recv()
            total = total + buf3[step - 1]
        own = pl.ds(own_at, own_rows)
        for c in range(2):
            modes_out[c, own, :] = modes_ref[c, own, :] + total[c] / (total[2] + 1.0)
        first = take(cols_n - 1)
        back_cols = []
        for step in range(1, cols_n):
            part = modes_out.at[:, own, :]
            back_cols.append(copy(part, part, (row, lax.rem(col + step, cols_n)), first + step - 1))
            back_cols[-1].start()
        finishing += [c.wait_send for c in back_cols]

    if has_halo:
        arrive()
        for c in range(2):
            ext_ref[2 * c, margin:tile_end, :] = jnp.where(upper, q_s[c], qlow_s[c])
            ext_ref[2 * c + 1, margin:tile_end, :] = jnp.where(upper, qhigh_s[c], q_s[c])

        @pl.when(row == 0)
        def _():
            ext_ref[:, :margin, :] = jnp.zeros((4, margin, size), jnp.float32)

        @pl.when(row == rows_n - 1)
        def _():
            ext_ref[:, tile_end:, :] = jnp.zeros((4, margin, size), jnp.float32)

        start, arrive, finish = edge_copies(
            ext_ref.at[:, pl.ds(margin, margin), :], ext_ref.at[:, pl.ds(tile_end, margin), :],
            ext_ref.at[:, pl.ds(size, margin), :], ext_ref.at[:, pl.ds(0, margin), :],
            "row", (send_sem, recv_sem, take(2)),
        )
        start()
        finishing.append(finish)

    if has_fold:
        for c in back_cols:
            c.wait_recv()
        first = take(lines - 1)
        back_lines = []
        for step in range(1, lines):
            part = modes_out.at[:, pl.ds(line_at, line_rows), :]
            to = lax.rem(line + step, lines)
            back_lines.append(copy(part, part, (to * 2 + core, col), first + step - 1))
            back_lines[-1].start()
        for c in back_lines:
            c.wait_recv()
        part = modes_out.at[:, pl.ds(half_at, half_rows), :]
        pair = copy(part, part, partner, take(1))
        pair.start()
        pair.wait_recv()
        finishing += [c.wait_send for c in back_lines + [pair]]
    if has_halo:
        arrive()
    for finish in finishing:
        finish()


def exchange_call(has_fold, has_halo, number, obj, acc=None, moments=None, modes=None):
    f32 = jnp.float32
    size = obj.shape[-1]
    margin = size // 2
    rows_n, cols_n = lax.axis_size("row"), lax.axis_size("col")
    vmem = pl.BlockSpec(memory_space=pltpu.VMEM)
    outs, scratch, inputs = [], [], [obj]
    sems = 0
    if has_fold:
        inputs += [acc, moments, modes]
        outs += [jax.ShapeDtypeStruct(obj.shape, f32), jax.ShapeDtypeStruct(modes.shape, f32)]
        sems += 6 + 2 * (rows_n // 2 - 1) + 2 * (cols_n - 1)
    if has_halo:
        outs.append(jax.ShapeDtypeStruct((4, 2 * size, size), f32))
        sems += 4
    scratch += [pltpu.SemaphoreType.DMA((sems,))] * 2
    if has_halo:
        scratch += [pltpu.VMEM((2, size, size), f32)] * 3
    if has_fold:
        half_rows = moments.shape[1] // 2
        lines = rows_n // 2
        line_rows = half_rows // lines
        own_rows = line_rows // cols_n
        scratch += [
            pltpu.VMEM((6, margin, size), f32),
            pltpu.VMEM((6, margin, size), f32),
            pltpu.VMEM((2, 3, size, size), f32),
            pltpu.VMEM((3, size, size), f32),
            pltpu.VMEM((3, size, size), f32),
            pltpu.VMEM((3, half_rows, size), f32),
            pltpu.VMEM((3, half_rows, size), f32),
            pltpu.VMEM((max(lines - 1, 1), 3, line_rows, size), f32),
            pltpu.VMEM((3, line_rows, size), f32),
            pltpu.VMEM((cols_n - 1, 3, own_rows, size), f32),
        ]
    return pl.pallas_call(
        functools.partial(exchange_kernel, has_fold, has_halo),
        out_shape=tuple(outs),
        in_specs=[vmem] * len(inputs),
        out_specs=(vmem,) * len(outs),
        scratch_shapes=scratch,
        compiler_params=pltpu.CompilerParams(
            collective_id=number, has_side_effects=True, vmem_limit_bytes=VMEM_LIMIT
        ),
        name=f"exchange{number}",
    )(*inputs)


def shards(object_field, probe_modes, coefficients, offsets, counts, measured):
    size = measured.shape[-1]
    kinds = probe_modes.shape[0]
    tables = dft_tables(size)
    coef = coefficients[0, 0]
    modes = probe_modes.transpose(1, 0, 2, 3)
    (ext,) = exchange_call(False, True, 0, object_field)
    for iteration in range(ITERS):
        acc, moments, num, den = positions_call(
            counts[0], offsets[0, 0], coef, ext.reshape(-1, size), modes, measured[0, 0], tables
        )
        coef = coef + num.sum(axis=-1) / (den.sum(axis=-1) + 1.0)
        more = iteration < ITERS - 1
        results = exchange_call(
            True, more, 1 if more else 2, object_field,
            acc.reshape(6, -1, size), moments.reshape(3, -1, size), modes.reshape(2, -1, size),
        )
        object_field, modes = results[0], results[1].reshape(2, kinds, size, size)
        if more:
            ext = results[2]
    return (object_field, modes.transpose(1, 0, 2, 3), coef[None, None])


def solution(mesh):
    placed = (
        P(None, "row", "col"),
        P(),
        P("row", "col", None, None),
        P("row", "col", None, None),
        P("row", "col"),
        P("row", "col", None, None, None),
    )
    return jax.shard_map(
        shards,
        mesh=mesh,
        in_specs=placed,
        out_specs=(P(None, "row", "col"), P(), P("row", "col", None, None)),
        check_vma=False,
    )
```

```python
import functools
import math

import jax
import jax.numpy as jnp
import numpy as np
from jax import lax
from jax.experimental import pallas as pl
from jax.experimental.pallas import tpu as pltpu
from jax.sharding import PartitionSpec as P

ITERS = 2
GROUP = 4
VMEM_LIMIT = 20 * 1024 * 1024

amp_floor = 0.5
count_scale = 0.03125


def halves(values):
    high = values.astype(jnp.bfloat16)
    low = (values - high.astype(jnp.float32)).astype(jnp.bfloat16)
    return high, low


def dft_tables(length):
    ramp = np.arange(length)
    angles = (ramp[:, None] * ramp[None, :] % length) * (2.0 * math.pi / length)
    cos = np.cos(angles) / math.sqrt(length)
    sin = -np.sin(angles) / math.sqrt(length)
    tables = []
    for part in (sin, -sin):
        right = jnp.asarray(np.block([[cos, part], [-part, cos]]), jnp.float32)
        left = jnp.asarray(np.block([[cos, -part], [part, cos]]), jnp.float32)
        high, low = halves(right)
        tables.append(jnp.concatenate([high, low, high], axis=0))
        high, low = halves(left)
        tables.append(jnp.concatenate([high, low, high], axis=1))
    return tables


def right_apply(values, table):
    high, low = halves(values)
    return jnp.dot(
        jnp.concatenate([high, high, low], axis=1), table, preferred_element_type=jnp.float32
    )


def left_apply(table, values):
    high, low = halves(values)
    return jnp.dot(
        table, jnp.concatenate([high, high, low], axis=0), preferred_element_type=jnp.float32
    )


def positions_kernel(
    count_ref, offs_ref, coef_ref, ext_ref, modes_ref, photon_ref, fr_ref, fl_ref, br_ref, bl_ref,
    acc_ref, mom_ref, num_ref, den_ref, obj_s, prb_s, psi_s, cross_s, power_s,
):
    _, modes, size, _ = modes_ref.shape
    extent = 2 * size
    step = 16
    chunks = size // step
    acc_ref[...] = jnp.zeros_like(acc_ref)
    mom_ref[...] = jnp.zeros_like(mom_ref)
    num_ref[...] = jnp.zeros_like(num_ref)
    den_ref[...] = jnp.zeros_like(den_ref)
    for k in range(modes):
        re, im = modes_ref[0, k], modes_ref[1, k]
        power_s[k] = re * re + im * im
    lane = lax.broadcasted_iota(jnp.int32, (size, size), 1)
    live = count_ref[0]

    def group(number, carry):
        first = number * GROUP
        weights = [[coef_ref[first + g, k] for k in range(modes)] for g in range(GROUP)]
        gates = [jnp.where(first + g < live, 1.0, 0.0).astype(jnp.float32) for g in range(GROUP)]
        corners = [(offs_ref[first + g, 0], offs_ref[first + g, 1]) for g in range(GROUP)]

        def probe_rows(chunk, carry):
            rows = pl.ds(pl.multiple_of(chunk * 8, 8), 8)
            for comp in range(2):
                parts = [modes_ref[comp, k, rows, :] for k in range(modes)]
                for g in range(GROUP):
                    total = weights[g][0] * parts[0]
                    for k in range(1, modes):
                        total = total + weights[g][k] * parts[k]
                    prb_s[g, comp, rows, :] = total
            return carry

        lax.fori_loop(0, size // 8, probe_rows, 0, unroll=2)

        for g in range(GROUP):
            top, left = corners[g]
            for comp in range(2):
                low = ext_ref[pl.ds(2 * comp * extent + top, size), :]
                high = ext_ref[pl.ds((2 * comp + 1) * extent + top, size), :]
                picked = jnp.where(lane >= left, low, high)
                obj_s[g, comp] = pltpu.roll(picked, lax.rem(size - left, size), 1)
            pr, pi, ore, oim = prb_s[g, 0], prb_s[g, 1], obj_s[g, 0], obj_s[g, 1]
            psi_s[g, :, :size] = pr * ore - pi * oim
            psi_s[g, :, size:] = pr * oim + pi * ore

        rowed = right_apply(psi_s[...].reshape(GROUP * size, 2 * size), fr_ref[...])
        for pair in range(GROUP // 2):
            one = rowed[2 * pair * size : (2 * pair + 1) * size]
            two = rowed[(2 * pair + 1) * size : (2 * pair + 2) * size]
            stacked = jnp.concatenate(
                [
                    jnp.concatenate([one[:, :size], two[:, :size]], axis=1),
                    jnp.concatenate([one[:, size:], two[:, size:]], axis=1),
                ],
                axis=0,
            )
            far = left_apply(fl_ref[...], stacked)
            far_real, far_imag = far[:size], far[size:]
            photons = jnp.concatenate(
                [photon_ref[first + 2 * pair], photon_ref[first + 2 * pair + 1]], axis=1
            )
            target = jnp.sqrt(photons.astype(jnp.float32)) * count_scale
            square = far_real * far_real + far_imag * far_imag
            scaling = target * lax.rsqrt(jnp.maximum(square, amp_floor * amp_floor))
            fixed = jnp.concatenate([far_real * scaling, far_imag * scaling], axis=0)
            near = left_apply(bl_ref[...], fixed)
            for half in range(2):
                g = 2 * pair + half
                cols = slice(half * size, (half + 1) * size)
                mixed = jnp.concatenate([near[:size, cols], near[size:, cols]], axis=1)
                back = right_apply(mixed, br_ref[...])
                diff = (back - psi_s[g]) * gates[g]
                dr, di = diff[:, :size], diff[:, size:]
                pr, pi, ore, oim = prb_s[g, 0], prb_s[g, 1], obj_s[g, 0], obj_s[g, 1]
                cross_s[g, 0] = ore * dr + oim * di
                cross_s[g, 1] = ore * di - oim * dr
                cross_s[g, 2] = (ore * ore + oim * oim) * gates[g]
                top, left = corners[g]
                pieces = (
                    pr * dr + pi * di,
                    pr * di - pi * dr,
                    (pr * pr + pi * pi) * gates[g],
                )
                inside = lane >= left
                for comp in range(3):
                    moved = pltpu.roll(pieces[comp], lax.rem(left, size), 1)
                    low = pl.ds(2 * comp * extent + top, size)
                    high = pl.ds((2 * comp + 1) * extent + top, size)
                    acc_ref[low, :] += jnp.where(inside, moved, 0.0)
                    acc_ref[high, :] += jnp.where(inside, 0.0, moved)

        def mode_sums(k, carry):
            used = [coef_ref[first + g, k] for g in range(GROUP)]

            def rows_sums(chunk, sums):
                rows = pl.ds(pl.multiple_of(chunk * step, step), step)
                re, im, power = modes_ref[0, k, rows, :], modes_ref[1, k, rows, :], power_s[k, rows, :]
                totals = [mom_ref[c, k, rows, :] for c in range(3)]
                new = []
                for g in range(GROUP):
                    cr, ci, cp = (cross_s[g, c, rows, :] for c in range(3))
                    totals[0] = totals[0] + used[g] * cr
                    totals[1] = totals[1] + used[g] * ci
                    totals[2] = totals[2] + (used[g] * used[g]) * cp
                    num = (cr * re + ci * im).reshape(step // 8, 8, size).sum(axis=0)
                    den = (cp * power).reshape(step // 8, 8, size).sum(axis=0)
                    new.append((sums[g][0] + num, sums[g][1] + den))
                for c in range(3):
                    mom_ref[c, k, rows, :] = totals[c]
                return tuple(new)

            zero = jnp.zeros((8, size), jnp.float32)
            sums = lax.fori_loop(
                0, chunks, rows_sums, tuple((zero, zero) for _ in range(GROUP)), unroll=4
            )
            for g in range(GROUP):
                num_ref[first + g, pl.ds(k, 1), :] = sums[g][0].sum(axis=0, keepdims=True)
                den_ref[first + g, pl.ds(k, 1), :] = sums[g][1].sum(axis=0, keepdims=True)
            return carry

        lax.fori_loop(0, modes, mode_sums, 0)
        return carry

    lax.fori_loop(0, (live + GROUP - 1) // GROUP, group, 0)


def positions_call(count, offs, coef, ext, modes, photons, tables):
    slots, kinds = coef.shape
    size = modes.shape[-1]
    extent = 2 * size
    smem = pl.BlockSpec(memory_space=pltpu.SMEM)
    vmem = pl.BlockSpec(memory_space=pltpu.VMEM)
    f32 = jnp.float32
    return pl.pallas_call(
        positions_kernel,
        out_shape=(
            jax.ShapeDtypeStruct((6 * extent, size), f32),
            jax.ShapeDtypeStruct((3, kinds, size, size), f32),
            jax.ShapeDtypeStruct((slots, kinds, size), f32),
            jax.ShapeDtypeStruct((slots, kinds, size), f32),
        ),
        in_specs=[smem] * 3 + [vmem] * 7,
        out_specs=(vmem,) * 4,
        scratch_shapes=[
            pltpu.VMEM((GROUP, 2, size, size), f32),
            pltpu.VMEM((GROUP, 2, size, size), f32),
            pltpu.VMEM((GROUP, size, 2 * size), f32),
            pltpu.VMEM((GROUP, 3, size, size), f32),
            pltpu.VMEM((kinds, size, size), f32),
        ],
        compiler_params=pltpu.CompilerParams(vmem_limit_bytes=VMEM_LIMIT),
        name="positions",
    )(count, offs, coef, ext, modes, photons, *tables)


def edge_copies(src_low, dst_low, src_high, dst_high, axis, sems):
    place = {name: lax.axis_index(name) for name in ("row", "col")}
    here, count = place[axis], lax.axis_size(axis)
    send_sem, recv_sem, first = sems
    copies = []
    for number, (src, dst, to) in enumerate(
        ((src_low, dst_low, jnp.maximum(here - 1, 0)), (src_high, dst_high, jnp.minimum(here + 1, count - 1)))
    ):
        target = dict(place)
        target[axis] = to
        copies.append(
            pltpu.make_async_remote_copy(
                src_ref=src,
                dst_ref=dst,
                send_sem=send_sem.at[first + number],
                recv_sem=recv_sem.at[first + number],
                device_id=(target["row"], target["col"]),
                device_id_type=pl.DeviceIdType.MESH,
            )
        )
    below, above = here > 0, here < count - 1

    def start():
        pl.when(below)(copies[0].start)
        pl.when(above)(copies[1].start)

    def arrive():
        pl.when(above)(copies[0].wait_recv)
        pl.when(below)(copies[1].wait_recv)

    def finish():
        pl.when(below)(copies[0].wait_send)
        pl.when(above)(copies[1].wait_send)

    return start, arrive, finish


def exchange_kernel(has_fold, has_halo, *refs):
    refs = list(refs)
    obj_ref = refs.pop(0)
    if has_fold:
        acc_ref, mom_ref, modes_ref = refs[:3]
        obj_out, modes_out = refs[3:5]
        refs = refs[5:]
    if has_halo:
        ext_ref = refs.pop(0)
    send_sem, recv_sem = refs[:2]
    refs = refs[2:]
    if has_halo:
        q_s, qlow_s, qhigh_s = refs[:3]
        refs = refs[3:]
    if has_fold:
        up_s, down_s, mid_s, fromlow_s, fromhigh_s, buf1, sum1, buf2, sum2, buf3 = refs

    row, col = lax.axis_index("row"), lax.axis_index("col")
    rows_n, cols_n = lax.axis_size("row"), lax.axis_size("col")
    size = obj_ref.shape[-1]
    margin = size // 2
    tile_end = margin + size

    barrier = pltpu.get_barrier_semaphore()
    for step in range(1, rows_n):
        pl.semaphore_signal(
            barrier, inc=1, device_id=(lax.rem(row + step, rows_n), col), device_id_type=pl.DeviceIdType.MESH
        )
    for step in range(1, cols_n):
        pl.semaphore_signal(
            barrier, inc=1, device_id=(row, lax.rem(col + step, cols_n)), device_id_type=pl.DeviceIdType.MESH
        )
    pl.semaphore_wait(barrier, rows_n + cols_n - 2)

    used = [0]

    def take(count):
        first = used[0]
        used[0] += count
        return first

    def copy(src, dst, device, number):
        return pltpu.make_async_remote_copy(
            src_ref=src,
            dst_ref=dst,
            send_sem=send_sem.at[number],
            recv_sem=recv_sem.at[number],
            device_id=device,
            device_id_type=pl.DeviceIdType.MESH,
        )

    finishing = []
    lane = lax.broadcasted_iota(jnp.int32, (size, size), 1)
    upper = lane >= margin

    if has_fold:
        total_rows = mom_ref.shape[1]
        core, line, lines = lax.rem(row, 2), row // 2, rows_n // 2
        half_rows = total_rows // 2
        line_rows = half_rows // lines
        own_rows = line_rows // cols_n
        half_at = pl.multiple_of(core * half_rows, half_rows)
        other_at = pl.multiple_of((1 - core) * half_rows, half_rows)
        line_at = pl.multiple_of(half_at + line * line_rows, line_rows)
        own_at = pl.multiple_of(line_at + col * own_rows, own_rows)
        partner = (line * 2 + 1 - core, col)

        planes = (2, 0, 1)
        first = take(3)
        pairs = [
            copy(mom_ref.at[p, pl.ds(other_at, half_rows), :], buf1.at[p], partner, first + p) for p in range(3)
        ]
        for p in planes:
            pairs[p].start()
        start, arrive, finish = edge_copies(
            acc_ref.at[:, pl.ds(0, margin), :], down_s,
            acc_ref.at[:, pl.ds(tile_end, margin), :], up_s,
            "row", (send_sem, recv_sem, take(2)),
        )

        @pl.when(row == 0)
        def _():
            up_s[...] = jnp.zeros_like(up_s)

        @pl.when(row == rows_n - 1)
        def _():
            down_s[...] = jnp.zeros_like(down_s)

        @pl.when(col == 0)
        def _():
            fromlow_s[...] = jnp.zeros_like(fromlow_s)

        @pl.when(col == cols_n - 1)
        def _():
            fromhigh_s[...] = jnp.zeros_like(fromhigh_s)

        start()
        finishing += [finish] + [c.wait_send for c in pairs]

        line_copies = {}
        for p in planes:
            pairs[p].wait_recv()
            sum1[p] = mom_ref[p, pl.ds(half_at, half_rows), :] + buf1[p]
            first = take(lines - 1)
            for step in range(1, lines):
                to = lax.rem(line + step, lines)
                at = pl.multiple_of(to * line_rows, line_rows)
                line_copies[p, step] = copy(
                    sum1.at[p, pl.ds(at, line_rows), :], buf2.at[step - 1, p], (to * 2 + core, col), first + step - 1
                )
                line_copies[p, step].start()

        arrive()
        for comp in range(3):
            for half in range(2):
                plane = 2 * comp + half
                mid_s[half, comp, :margin, :] = acc_ref[plane, margin:size, :] + up_s[plane]
                mid_s[half, comp, margin:, :] = acc_ref[plane, size:tile_end, :] + down_s[plane]
        start, arrive, finish = edge_copies(
            mid_s.at[0], fromhigh_s, mid_s.at[1], fromlow_s, "col", (send_sem, recv_sem, take(2))
        )
        start()
        finishing.append(finish)

        col_copies = {}
        for p in planes:
            total = sum1[p, pl.ds(pl.multiple_of(line * line_rows, line_rows), line_rows), :]
            for step in range(1, lines):
                line_copies[p, step].wait_recv()
                total = total + buf2[step - 1, p]
            sum2[p] = total
            first = take(cols_n - 1)
            for step in range(1, cols_n):
                to = lax.rem(col + step, cols_n)
                at = pl.multiple_of(to * own_rows, own_rows)
                col_copies[p, step] = copy(
                    sum2.at[p, pl.ds(at, own_rows), :], buf3.at[step - 1, p], (row, to), first + step - 1
                )
                col_copies[p, step].start()
        finishing += [c.wait_send for c in (*line_copies.values(), *col_copies.values())]

        arrive()
        parts = [
            jnp.where(upper, mid_s[0, c] + fromlow_s[c], mid_s[1, c] + fromhigh_s[c]) for c in range(3)
        ]
        for c in range(2):
            new = pltpu.roll(obj_ref[c], margin, 1) + parts[c] / (parts[2] + 1.0)
            if has_halo:
                q_s[c] = new
            obj_out[c] = pltpu.roll(new, margin, 1)
    else:
        for c in range(2):
            q_s[c] = pltpu.roll(obj_ref[c], margin, 1)

    if has_halo:

        @pl.when(col == 0)
        def _():
            qlow_s[...] = jnp.zeros_like(qlow_s)

        @pl.when(col == cols_n - 1)
        def _():
            qhigh_s[...] = jnp.zeros_like(qhigh_s)

        start, arrive, finish = edge_copies(q_s, qhigh_s, q_s, qlow_s, "col", (send_sem, recv_sem, take(2)))
        start()
        finishing.append(finish)

    if has_fold:
        own = pl.ds(own_at, own_rows)
        back_cols = {}
        for p in planes:
            total = sum2[p, pl.ds(pl.multiple_of(col * own_rows, own_rows), own_rows), :]
            for step in range(1, cols_n):
                col_copies[p, step].wait_recv()
                total = total + buf3[step - 1, p]
            if p == 2:
                below = total + 1.0
                continue
            modes_out[p, own, :] = modes_ref[p, own, :] + total / below
            first = take(cols_n - 1)
            for step in range(1, cols_n):
                part = modes_out.at[p, own, :]
                back_cols[p, step] = copy(part, part, (row, lax.rem(col + step, cols_n)), first + step - 1)
                back_cols[p, step].start()
        finishing += [c.wait_send for c in back_cols.values()]

    if has_halo:
        arrive()
        for c in range(2):
            ext_ref[2 * c, margin:tile_end, :] = jnp.where(upper, q_s[c], qlow_s[c])
            ext_ref[2 * c + 1, margin:tile_end, :] = jnp.where(upper, qhigh_s[c], q_s[c])

        @pl.when(row == 0)
        def _():
            ext_ref[:, :margin, :] = jnp.zeros((4, margin, size), jnp.float32)

        @pl.when(row == rows_n - 1)
        def _():
            ext_ref[:, tile_end:, :] = jnp.zeros((4, margin, size), jnp.float32)

        start, arrive, finish = edge_copies(
            ext_ref.at[:, pl.ds(margin, margin), :], ext_ref.at[:, pl.ds(tile_end, margin), :],
            ext_ref.at[:, pl.ds(size, margin), :], ext_ref.at[:, pl.ds(0, margin), :],
            "row", (send_sem, recv_sem, take(2)),
        )
        start()
        finishing.append(finish)

    if has_fold:
        back_lines, back_pairs = {}, []
        for c in range(2):
            for step in range(1, cols_n):
                back_cols[c, step].wait_recv()
            first = take(lines - 1)
            for step in range(1, lines):
                part = modes_out.at[c, pl.ds(line_at, line_rows), :]
                to = lax.rem(line + step, lines)
                back_lines[c, step] = copy(part, part, (to * 2 + core, col), first + step - 1)
                back_lines[c, step].start()
        for c in range(2):
            for step in range(1, lines):
                back_lines[c, step].wait_recv()
            part = modes_out.at[c, pl.ds(half_at, half_rows), :]
            back_pairs.append(copy(part, part, partner, take(1)))
            back_pairs[-1].start()
        for pair in back_pairs:
            pair.wait_recv()
        finishing += [c.wait_send for c in (*back_lines.values(), *back_pairs)]
    if has_halo:
        arrive()
    for finish in finishing:
        finish()


def exchange_call(has_fold, has_halo, number, obj, acc=None, moments=None, modes=None):
    f32 = jnp.float32
    size = obj.shape[-1]
    margin = size // 2
    rows_n, cols_n = lax.axis_size("row"), lax.axis_size("col")
    vmem = pl.BlockSpec(memory_space=pltpu.VMEM)
    outs, scratch, inputs = [], [], [obj]
    sems = 0
    if has_fold:
        inputs += [acc, moments, modes]
        outs += [jax.ShapeDtypeStruct(obj.shape, f32), jax.ShapeDtypeStruct(modes.shape, f32)]
        sems += 4 + 5 * (1 + rows_n // 2 - 1 + cols_n - 1)
    if has_halo:
        outs.append(jax.ShapeDtypeStruct((4, 2 * size, size), f32))
        sems += 4
    scratch += [pltpu.SemaphoreType.DMA((sems,))] * 2
    if has_halo:
        scratch += [pltpu.VMEM((2, size, size), f32)] * 3
    if has_fold:
        half_rows = moments.shape[1] // 2
        lines = rows_n // 2
        line_rows = half_rows // lines
        own_rows = line_rows // cols_n
        scratch += [
            pltpu.VMEM((6, margin, size), f32),
            pltpu.VMEM((6, margin, size), f32),
            pltpu.VMEM((2, 3, size, size), f32),
            pltpu.VMEM((3, size, size), f32),
            pltpu.VMEM((3, size, size), f32),
            pltpu.VMEM((3, half_rows, size), f32),
            pltpu.VMEM((3, half_rows, size), f32),
            pltpu.VMEM((max(lines - 1, 1), 3, line_rows, size), f32),
            pltpu.VMEM((3, line_rows, size), f32),
            pltpu.VMEM((cols_n - 1, 3, own_rows, size), f32),
        ]
    return pl.pallas_call(
        functools.partial(exchange_kernel, has_fold, has_halo),
        out_shape=tuple(outs),
        in_specs=[vmem] * len(inputs),
        out_specs=(vmem,) * len(outs),
        scratch_shapes=scratch,
        compiler_params=pltpu.CompilerParams(
            collective_id=number, has_side_effects=True, vmem_limit_bytes=VMEM_LIMIT
        ),
        name=f"exchange{number}",
    )(*inputs)


def shards(object_field, probe_modes, coefficients, offsets, counts, measured):
    size = measured.shape[-1]
    kinds = probe_modes.shape[0]
    tables = dft_tables(size)
    coef = coefficients[0, 0]
    modes = probe_modes.transpose(1, 0, 2, 3)
    (ext,) = exchange_call(False, True, 0, object_field)
    for iteration in range(ITERS):
        acc, moments, num, den = positions_call(
            counts[0], offsets[0, 0], coef, ext.reshape(-1, size), modes, measured[0, 0], tables
        )
        coef = coef + num.sum(axis=-1) / (den.sum(axis=-1) + 1.0)
        more = iteration < ITERS - 1
        results = exchange_call(
            True, more, 1 if more else 2, object_field,
            acc.reshape(6, -1, size), moments.reshape(3, -1, size), modes.reshape(2, -1, size),
        )
        object_field, modes = results[0], results[1].reshape(2, kinds, size, size)
        if more:
            ext = results[2]
    return (object_field, modes.transpose(1, 0, 2, 3), coef[None, None])


def solution(mesh):
    placed = (
        P(None, "row", "col"),
        P(),
        P("row", "col", None, None),
        P("row", "col", None, None),
        P("row", "col"),
        P("row", "col", None, None, None),
    )
    return jax.shard_map(
        shards,
        mesh=mesh,
        in_specs=placed,
        out_specs=(P(None, "row", "col"), P(), P("row", "col", None, None)),
        check_vma=False,
    )
```

```python
import functools
import math

import jax
import jax.numpy as jnp
import numpy as np
from jax import lax
from jax.experimental import pallas as pl
from jax.experimental.pallas import tpu as pltpu
from jax.sharding import PartitionSpec as P

ITERS = 2
GROUP = 4
VMEM_LIMIT = 48 * 1024 * 1024

amp_floor = 0.5
count_scale = 0.03125


def halves(values):
    high = values.astype(jnp.bfloat16)
    low = (values - high.astype(jnp.float32)).astype(jnp.bfloat16)
    return high, low


def dft_tables(length):
    ramp = np.arange(length)
    angles = (ramp[:, None] * ramp[None, :] % length) * (2.0 * math.pi / length)
    cos = np.cos(angles) / math.sqrt(length)
    sin = -np.sin(angles) / math.sqrt(length)
    tables = []
    for part in (sin, -sin):
        right = jnp.asarray(np.block([[cos, part], [-part, cos]]), jnp.float32)
        left = jnp.asarray(np.block([[cos, -part], [part, cos]]), jnp.float32)
        high, low = halves(right)
        tables.append(jnp.concatenate([high, low, high], axis=0))
        high, low = halves(left)
        tables.append(jnp.concatenate([high, low, high], axis=1))
    return tables


def right_apply(values, table):
    high, low = halves(values)
    return jnp.dot(
        jnp.concatenate([high, high, low], axis=1), table, preferred_element_type=jnp.float32
    )


def left_apply(table, values):
    high, low = halves(values)
    return jnp.dot(
        table, jnp.concatenate([high, high, low], axis=0), preferred_element_type=jnp.float32
    )


def positions_kernel(
    count_ref, offs_ref, coef_ref, ext_ref, modes_ref, photon_ref, fr_ref, fl_ref, br_ref, bl_ref,
    acc_ref, mom_ref, num_ref, den_ref, obj_s, prb_s, psi_s, cross_s, power_s,
):
    _, modes, size, _ = modes_ref.shape
    extent = 2 * size
    step = 16
    chunks = size // step
    acc_ref[...] = jnp.zeros_like(acc_ref)
    mom_ref[...] = jnp.zeros_like(mom_ref)
    num_ref[...] = jnp.zeros_like(num_ref)
    den_ref[...] = jnp.zeros_like(den_ref)
    for k in range(modes):
        re, im = modes_ref[0, k], modes_ref[1, k]
        power_s[k] = re * re + im * im
    lane = lax.broadcasted_iota(jnp.int32, (size, size), 1)
    live = count_ref[0]

    def group(number, carry):
        first = number * GROUP
        weights = [[coef_ref[first + g, k] for k in range(modes)] for g in range(GROUP)]
        gates = [jnp.where(first + g < live, 1.0, 0.0).astype(jnp.float32) for g in range(GROUP)]
        corners = [(offs_ref[first + g, 0], offs_ref[first + g, 1]) for g in range(GROUP)]

        def probe_rows(chunk, carry):
            rows = pl.ds(pl.multiple_of(chunk * 8, 8), 8)
            for comp in range(2):
                parts = [modes_ref[comp, k, rows, :] for k in range(modes)]
                for g in range(GROUP):
                    total = weights[g][0] * parts[0]
                    for k in range(1, modes):
                        total = total + weights[g][k] * parts[k]
                    prb_s[g, comp, rows, :] = total
            return carry

        lax.fori_loop(0, size // 8, probe_rows, 0, unroll=2)

        for g in range(GROUP):
            top, left = corners[g]
            for comp in range(2):
                low = ext_ref[pl.ds(2 * comp * extent + top, size), :]
                high = ext_ref[pl.ds((2 * comp + 1) * extent + top, size), :]
                picked = jnp.where(lane >= left, low, high)
                obj_s[g, comp] = pltpu.roll(picked, lax.rem(size - left, size), 1)
            pr, pi, ore, oim = prb_s[g, 0], prb_s[g, 1], obj_s[g, 0], obj_s[g, 1]
            psi_s[g, :, :size] = pr * ore - pi * oim
            psi_s[g, :, size:] = pr * oim + pi * ore

        rowed = right_apply(psi_s[...].reshape(GROUP * size, 2 * size), fr_ref[...])
        for pair in range(GROUP // 2):
            one = rowed[2 * pair * size : (2 * pair + 1) * size]
            two = rowed[(2 * pair + 1) * size : (2 * pair + 2) * size]
            stacked = jnp.concatenate(
                [
                    jnp.concatenate([one[:, :size], two[:, :size]], axis=1),
                    jnp.concatenate([one[:, size:], two[:, size:]], axis=1),
                ],
                axis=0,
            )
            far = left_apply(fl_ref[...], stacked)
            far_real, far_imag = far[:size], far[size:]
            photons = jnp.concatenate(
                [photon_ref[first + 2 * pair], photon_ref[first + 2 * pair + 1]], axis=1
            )
            target = jnp.sqrt(photons.astype(jnp.float32)) * count_scale
            square = far_real * far_real + far_imag * far_imag
            scaling = target * lax.rsqrt(jnp.maximum(square, amp_floor * amp_floor))
            fixed = jnp.concatenate([far_real * scaling, far_imag * scaling], axis=0)
            near = left_apply(bl_ref[...], fixed)
            for half in range(2):
                g = 2 * pair + half
                cols = slice(half * size, (half + 1) * size)
                mixed = jnp.concatenate([near[:size, cols], near[size:, cols]], axis=1)
                back = right_apply(mixed, br_ref[...])
                diff = (back - psi_s[g]) * gates[g]
                dr, di = diff[:, :size], diff[:, size:]
                pr, pi, ore, oim = prb_s[g, 0], prb_s[g, 1], obj_s[g, 0], obj_s[g, 1]
                cross_s[g, 0] = ore * dr + oim * di
                cross_s[g, 1] = ore * di - oim * dr
                cross_s[g, 2] = (ore * ore + oim * oim) * gates[g]
                top, left = corners[g]
                pieces = (
                    pr * dr + pi * di,
                    pr * di - pi * dr,
                    (pr * pr + pi * pi) * gates[g],
                )
                inside = lane >= left
                for comp in range(3):
                    moved = pltpu.roll(pieces[comp], lax.rem(left, size), 1)
                    low = pl.ds(2 * comp * extent + top, size)
                    high = pl.ds((2 * comp + 1) * extent + top, size)
                    acc_ref[low, :] += jnp.where(inside, moved, 0.0)
                    acc_ref[high, :] += jnp.where(inside, 0.0, moved)

        def mode_sums(k, carry):
            used = [coef_ref[first + g, k] for g in range(GROUP)]

            def rows_sums(chunk, sums):
                rows = pl.ds(pl.multiple_of(chunk * step, step), step)
                re, im, power = modes_ref[0, k, rows, :], modes_ref[1, k, rows, :], power_s[k, rows, :]
                totals = [mom_ref[c, k, rows, :] for c in range(3)]
                new = []
                for g in range(GROUP):
                    cr, ci, cp = (cross_s[g, c, rows, :] for c in range(3))
                    totals[0] = totals[0] + used[g] * cr
                    totals[1] = totals[1] + used[g] * ci
                    totals[2] = totals[2] + (used[g] * used[g]) * cp
                    num = (cr * re + ci * im).reshape(step // 8, 8, size).sum(axis=0)
                    den = (cp * power).reshape(step // 8, 8, size).sum(axis=0)
                    new.append((sums[g][0] + num, sums[g][1] + den))
                for c in range(3):
                    mom_ref[c, k, rows, :] = totals[c]
                return tuple(new)

            zero = jnp.zeros((8, size), jnp.float32)
            sums = lax.fori_loop(
                0, chunks, rows_sums, tuple((zero, zero) for _ in range(GROUP)), unroll=4
            )
            for g in range(GROUP):
                num_ref[first + g, pl.ds(k, 1), :] = sums[g][0].sum(axis=0, keepdims=True)
                den_ref[first + g, pl.ds(k, 1), :] = sums[g][1].sum(axis=0, keepdims=True)
            return carry

        lax.fori_loop(0, modes, mode_sums, 0)
        return carry

    lax.fori_loop(0, (live + GROUP - 1) // GROUP, group, 0)


def positions_call(count, offs, coef, ext, modes, photons, tables):
    slots, kinds = coef.shape
    size = modes.shape[-1]
    extent = 2 * size
    smem = pl.BlockSpec(memory_space=pltpu.SMEM)
    vmem = pl.BlockSpec(memory_space=pltpu.VMEM)
    f32 = jnp.float32
    return pl.pallas_call(
        positions_kernel,
        out_shape=(
            jax.ShapeDtypeStruct((6 * extent, size), f32),
            jax.ShapeDtypeStruct((3, kinds, size, size), f32),
            jax.ShapeDtypeStruct((slots, kinds, size), f32),
            jax.ShapeDtypeStruct((slots, kinds, size), f32),
        ),
        in_specs=[smem] * 3 + [vmem] * 7,
        out_specs=(vmem,) * 4,
        scratch_shapes=[
            pltpu.VMEM((GROUP, 2, size, size), f32),
            pltpu.VMEM((GROUP, 2, size, size), f32),
            pltpu.VMEM((GROUP, size, 2 * size), f32),
            pltpu.VMEM((GROUP, 3, size, size), f32),
            pltpu.VMEM((kinds, size, size), f32),
        ],
        compiler_params=pltpu.CompilerParams(vmem_limit_bytes=VMEM_LIMIT),
        name="positions",
    )(count, offs, coef, ext, modes, photons, *tables)


def pack(values, upper_half):
    size = values.shape[-1]
    margin = size // 2
    first, last = values[:margin], pltpu.roll(values[margin:], margin, 1)
    upper = lax.broadcasted_iota(jnp.int32, (margin, size), 1) >= margin
    return jnp.where(upper, first, last) if upper_half else jnp.where(upper, last, first)


def unpack(packed):
    return jnp.concatenate([packed, pltpu.roll(packed, packed.shape[-1] // 2, 1)], axis=0)


def edge_copies(src_low, dst_low, src_high, dst_high, axis, sems):
    place = {name: lax.axis_index(name) for name in ("row", "col")}
    here, count = place[axis], lax.axis_size(axis)
    send_sem, recv_sem, first = sems
    copies = []
    for number, (src, dst, to) in enumerate(
        ((src_low, dst_low, jnp.maximum(here - 1, 0)), (src_high, dst_high, jnp.minimum(here + 1, count - 1)))
    ):
        target = dict(place)
        target[axis] = to
        copies.append(
            pltpu.make_async_remote_copy(
                src_ref=src,
                dst_ref=dst,
                send_sem=send_sem.at[first + number],
                recv_sem=recv_sem.at[first + number],
                device_id=(target["row"], target["col"]),
                device_id_type=pl.DeviceIdType.MESH,
            )
        )
    below, above = here > 0, here < count - 1

    def start():
        pl.when(below)(copies[0].start)
        pl.when(above)(copies[1].start)

    def arrive():
        pl.when(above)(copies[0].wait_recv)
        pl.when(below)(copies[1].wait_recv)

    def finish():
        pl.when(below)(copies[0].wait_send)
        pl.when(above)(copies[1].wait_send)

    return start, arrive, finish


def exchange_kernel(has_fold, has_halo, *refs):
    refs = list(refs)
    obj_ref = refs.pop(0)
    if has_fold:
        acc_ref, mom_ref, modes_ref = refs[:3]
        obj_out, modes_out = refs[3:5]
        refs = refs[5:]
    if has_halo:
        ext_ref = refs.pop(0)
    send_sem, recv_sem = refs[:2]
    refs = refs[2:]
    if has_halo:
        q_s, qsend_s, qlow_s, qhigh_s = refs[:4]
        refs = refs[4:]
    if has_fold:
        up_s, down_s, mid_s, midsend_s, fromlow_s, fromhigh_s, buf1, sum1, buf2, sum2, buf3 = refs

    row, col = lax.axis_index("row"), lax.axis_index("col")
    rows_n, cols_n = lax.axis_size("row"), lax.axis_size("col")
    size = obj_ref.shape[-1]
    margin = size // 2
    tile_end = margin + size

    barrier = pltpu.get_barrier_semaphore()
    for step in range(1, rows_n):
        pl.semaphore_signal(
            barrier, inc=1, device_id=(lax.rem(row + step, rows_n), col), device_id_type=pl.DeviceIdType.MESH
        )
    for step in range(1, cols_n):
        pl.semaphore_signal(
            barrier, inc=1, device_id=(row, lax.rem(col + step, cols_n)), device_id_type=pl.DeviceIdType.MESH
        )
    pl.semaphore_wait(barrier, rows_n + cols_n - 2)

    used = [0]

    def take(count):
        first = used[0]
        used[0] += count
        return first

    def copy(src, dst, device, number):
        return pltpu.make_async_remote_copy(
            src_ref=src,
            dst_ref=dst,
            send_sem=send_sem.at[number],
            recv_sem=recv_sem.at[number],
            device_id=device,
            device_id_type=pl.DeviceIdType.MESH,
        )

    finishing = []
    lane = lax.broadcasted_iota(jnp.int32, (size, size), 1)
    upper = lane >= margin

    if has_fold:
        total_rows = mom_ref.shape[1]
        core, line, lines = lax.rem(row, 2), row // 2, rows_n // 2
        half_rows = total_rows // 2
        line_rows = half_rows // lines
        own_rows = line_rows // cols_n
        half_at = pl.multiple_of(core * half_rows, half_rows)
        other_at = pl.multiple_of((1 - core) * half_rows, half_rows)
        line_at = pl.multiple_of(half_at + line * line_rows, line_rows)
        own_at = pl.multiple_of(line_at + col * own_rows, own_rows)
        partner = (line * 2 + 1 - core, col)

        planes = (2, 0, 1)
        first = take(3)
        pairs = [
            copy(mom_ref.at[p, pl.ds(other_at, half_rows), :], buf1.at[p], partner, first + p) for p in range(3)
        ]
        for p in planes:
            pairs[p].start()
        start, arrive, finish = edge_copies(
            acc_ref.at[:, pl.ds(0, margin), :], down_s,
            acc_ref.at[:, pl.ds(tile_end, margin), :], up_s,
            "row", (send_sem, recv_sem, take(2)),
        )

        @pl.when(row == 0)
        def _():
            up_s[...] = jnp.zeros_like(up_s)

        @pl.when(row == rows_n - 1)
        def _():
            down_s[...] = jnp.zeros_like(down_s)

        @pl.when(col == 0)
        def _():
            fromlow_s[...] = jnp.zeros_like(fromlow_s)

        @pl.when(col == cols_n - 1)
        def _():
            fromhigh_s[...] = jnp.zeros_like(fromhigh_s)

        start()
        finishing += [finish] + [c.wait_send for c in pairs]

        line_copies = {}
        for p in planes:
            pairs[p].wait_recv()
            sum1[p] = mom_ref[p, pl.ds(half_at, half_rows), :] + buf1[p]
            first = take(lines - 1)
            for step in range(1, lines):
                to = lax.rem(line + step, lines)
                at = pl.multiple_of(to * line_rows, line_rows)
                line_copies[p, step] = copy(
                    sum1.at[p, pl.ds(at, line_rows), :], buf2.at[step - 1, p], (to * 2 + core, col), first + step - 1
                )
                line_copies[p, step].start()

        arrive()
        for comp in range(3):
            for half in range(2):
                plane = 2 * comp + half
                mid_s[half, comp, :margin, :] = acc_ref[plane, margin:size, :] + up_s[plane]
                mid_s[half, comp, margin:, :] = acc_ref[plane, size:tile_end, :] + down_s[plane]
            for half in range(2):
                midsend_s[half, comp] = pack(mid_s[half, comp], half == 1)
        start, arrive, finish = edge_copies(
            midsend_s.at[0], fromhigh_s, midsend_s.at[1], fromlow_s, "col", (send_sem, recv_sem, take(2))
        )
        start()
        finishing.append(finish)

        col_copies = {}
        for p in planes:
            total = sum1[p, pl.ds(pl.multiple_of(line * line_rows, line_rows), line_rows), :]
            for step in range(1, lines):
                line_copies[p, step].wait_recv()
                total = total + buf2[step - 1, p]
            sum2[p] = total
            first = take(cols_n - 1)
            for step in range(1, cols_n):
                to = lax.rem(col + step, cols_n)
                at = pl.multiple_of(to * own_rows, own_rows)
                col_copies[p, step] = copy(
                    sum2.at[p, pl.ds(at, own_rows), :], buf3.at[step - 1, p], (row, to), first + step - 1
                )
                col_copies[p, step].start()
        finishing += [c.wait_send for c in (*line_copies.values(), *col_copies.values())]

        arrive()
        parts = [
            jnp.where(upper, mid_s[0, c] + unpack(fromlow_s[c]), mid_s[1, c] + unpack(fromhigh_s[c]))
            for c in range(3)
        ]
        for c in range(2):
            new = pltpu.roll(obj_ref[c], margin, 1) + parts[c] / (parts[2] + 1.0)
            if has_halo:
                q_s[c] = new
            obj_out[c] = pltpu.roll(new, margin, 1)
    else:
        for c in range(2):
            q_s[c] = pltpu.roll(obj_ref[c], margin, 1)

    if has_halo:

        @pl.when(col == 0)
        def _():
            qlow_s[...] = jnp.zeros_like(qlow_s)

        @pl.when(col == cols_n - 1)
        def _():
            qhigh_s[...] = jnp.zeros_like(qhigh_s)

        for c in range(2):
            qsend_s[0, c] = pack(q_s[c], True)
            qsend_s[1, c] = pack(q_s[c], False)
        start, arrive, finish = edge_copies(
            qsend_s.at[0], qhigh_s, qsend_s.at[1], qlow_s, "col", (send_sem, recv_sem, take(2))
        )
        start()
        finishing.append(finish)

    if has_fold:
        own = pl.ds(own_at, own_rows)
        back_cols = {}
        for p in planes:
            total = sum2[p, pl.ds(pl.multiple_of(col * own_rows, own_rows), own_rows), :]
            for step in range(1, cols_n):
                col_copies[p, step].wait_recv()
                total = total + buf3[step - 1, p]
            if p == 2:
                below = total + 1.0
                continue
            modes_out[p, own, :] = modes_ref[p, own, :] + total / below
            first = take(cols_n - 1)
            for step in range(1, cols_n):
                part = modes_out.at[p, own, :]
                back_cols[p, step] = copy(part, part, (row, lax.rem(col + step, cols_n)), first + step - 1)
                back_cols[p, step].start()
        finishing += [c.wait_send for c in back_cols.values()]

    if has_halo:
        arrive()
        for c in range(2):
            ext_ref[2 * c, margin:tile_end, :] = jnp.where(upper, q_s[c], unpack(qlow_s[c]))
            ext_ref[2 * c + 1, margin:tile_end, :] = jnp.where(upper, unpack(qhigh_s[c]), q_s[c])

        @pl.when(row == 0)
        def _():
            ext_ref[:, :margin, :] = jnp.zeros((4, margin, size), jnp.float32)

        @pl.when(row == rows_n - 1)
        def _():
            ext_ref[:, tile_end:, :] = jnp.zeros((4, margin, size), jnp.float32)

        start, arrive, finish = edge_copies(
            ext_ref.at[:, pl.ds(margin, margin), :], ext_ref.at[:, pl.ds(tile_end, margin), :],
            ext_ref.at[:, pl.ds(size, margin), :], ext_ref.at[:, pl.ds(0, margin), :],
            "row", (send_sem, recv_sem, take(2)),
        )
        start()
        finishing.append(finish)

    if has_fold:
        back_lines, back_pairs = {}, []
        for c in range(2):
            for step in range(1, cols_n):
                back_cols[c, step].wait_recv()
            first = take(lines - 1)
            for step in range(1, lines):
                part = modes_out.at[c, pl.ds(line_at, line_rows), :]
                to = lax.rem(line + step, lines)
                back_lines[c, step] = copy(part, part, (to * 2 + core, col), first + step - 1)
                back_lines[c, step].start()
        for c in range(2):
            for step in range(1, lines):
                back_lines[c, step].wait_recv()
            part = modes_out.at[c, pl.ds(half_at, half_rows), :]
            back_pairs.append(copy(part, part, partner, take(1)))
            back_pairs[-1].start()
        for pair in back_pairs:
            pair.wait_recv()
        finishing += [c.wait_send for c in (*back_lines.values(), *back_pairs)]
    if has_halo:
        arrive()
    for finish in finishing:
        finish()


def exchange_call(has_fold, has_halo, number, obj, acc=None, moments=None, modes=None):
    f32 = jnp.float32
    size = obj.shape[-1]
    margin = size // 2
    rows_n, cols_n = lax.axis_size("row"), lax.axis_size("col")
    vmem = pl.BlockSpec(memory_space=pltpu.VMEM)
    outs, scratch, inputs = [], [], [obj]
    sems = 0
    if has_fold:
        inputs += [acc, moments, modes]
        outs += [jax.ShapeDtypeStruct(obj.shape, f32), jax.ShapeDtypeStruct(modes.shape, f32)]
        sems += 4 + 5 * (1 + rows_n // 2 - 1 + cols_n - 1)
    if has_halo:
        outs.append(jax.ShapeDtypeStruct((4, 2 * size, size), f32))
        sems += 4
    scratch += [pltpu.SemaphoreType.DMA((sems,))] * 2
    if has_halo:
        scratch += [
            pltpu.VMEM((2, size, size), f32),
            pltpu.VMEM((2, 2, margin, size), f32),
            pltpu.VMEM((2, margin, size), f32),
            pltpu.VMEM((2, margin, size), f32),
        ]
    if has_fold:
        half_rows = moments.shape[1] // 2
        lines = rows_n // 2
        line_rows = half_rows // lines
        own_rows = line_rows // cols_n
        scratch += [
            pltpu.VMEM((6, margin, size), f32),
            pltpu.VMEM((6, margin, size), f32),
            pltpu.VMEM((2, 3, size, size), f32),
            pltpu.VMEM((2, 3, margin, size), f32),
            pltpu.VMEM((3, margin, size), f32),
            pltpu.VMEM((3, margin, size), f32),
            pltpu.VMEM((3, half_rows, size), f32),
            pltpu.VMEM((3, half_rows, size), f32),
            pltpu.VMEM((max(lines - 1, 1), 3, line_rows, size), f32),
            pltpu.VMEM((3, line_rows, size), f32),
            pltpu.VMEM((cols_n - 1, 3, own_rows, size), f32),
        ]
    return pl.pallas_call(
        functools.partial(exchange_kernel, has_fold, has_halo),
        out_shape=tuple(outs),
        in_specs=[vmem] * len(inputs),
        out_specs=(vmem,) * len(outs),
        scratch_shapes=scratch,
        compiler_params=pltpu.CompilerParams(
            collective_id=number, has_side_effects=True, vmem_limit_bytes=VMEM_LIMIT
        ),
        name=f"exchange{number}",
    )(*inputs)


def shards(object_field, probe_modes, coefficients, offsets, counts, measured):
    size = measured.shape[-1]
    kinds = probe_modes.shape[0]
    tables = dft_tables(size)
    coef = coefficients[0, 0]
    modes = probe_modes.transpose(1, 0, 2, 3)
    (ext,) = exchange_call(False, True, 0, object_field)
    for iteration in range(ITERS):
        acc, moments, num, den = positions_call(
            counts[0], offsets[0, 0], coef, ext.reshape(-1, size), modes, measured[0, 0], tables
        )
        coef = coef + num.sum(axis=-1) / (den.sum(axis=-1) + 1.0)
        more = iteration < ITERS - 1
        results = exchange_call(
            True, more, 1 if more else 2, object_field,
            acc.reshape(6, -1, size), moments.reshape(3, -1, size), modes.reshape(2, -1, size),
        )
        object_field, modes = results[0], results[1].reshape(2, kinds, size, size)
        if more:
            ext = results[2]
    return (object_field, modes.transpose(1, 0, 2, 3), coef[None, None])


def solution(mesh):
    placed = (
        P(None, "row", "col"),
        P(),
        P("row", "col", None, None),
        P("row", "col", None, None),
        P("row", "col"),
        P("row", "col", None, None, None),
    )
    return jax.shard_map(
        shards,
        mesh=mesh,
        in_specs=placed,
        out_specs=(P(None, "row", "col"), P(), P("row", "col", None, None)),
        check_vma=False,
    )
```
